32 devices in a mesh: grp: 2 (over x), seq: 16 (over z, y, core).
Axes of the slice: x: 2, y: 2, z: 4, core: 2. Of those that a mesh axis runs over, the one named last changes fastest.
Arguments:
- tokens: bfloat16 [2, 131072, 768], P('grp', 'seq'), parts along dimension 0, may hold values from -36 to 36
- right_factor: bfloat16 [256, 512, 512], P('seq'), may hold values from -0.25 to 0.25
- left_factor: bfloat16 [512, 256, 256], P('seq'), may hold values from -0.375 to 0.375
- twiddle: float32 [256, 512], P('seq'), may hold values from 0.5 to 2
- norm_gain: float32 [768], replicated, may hold values from 0.1 to 1.9
- mix_gain: float32 [768], replicated, may hold values from 0.1 to 1.9
- value_weight: bfloat16 [768, 768], replicated, may hold values from -0.21875 to 0.21875
- gate_weight: bfloat16 [768, 768], replicated, may hold values from -0.21875 to 0.21875
Outputs:
- layer_out: bfloat16 [2, 131072, 768], P('grp', 'seq'), parts along dimension 0
The draws below stay inside these ranges and needn't reach their ends.
There are 2 independent parts, one for each index of `grp`. The reference program is written for one: setup_inputs(seed, part) draws one part's arguments, and reference() takes and returns one part's arrays. A program takes and returns all parts, laid end to end along the dimension named above; an argument that names none is the same for every part. Nothing has to cross between parts.
All inputs are finite; a program needn't handle non-finite values.
Results may differ from the reference program's by a relative error of at most 0.0051.
Values may be sent and summed in bfloat16 or wider, within the bound.
A program may use at most 192 MiB of HBM per device.

```python
import math
import jax
import jax.numpy as jnp
from jax import lax

C = 768
BLK = 512
NBLK = 256
SEQS = 1
L = 131072


def draw_tokens(key, part):
    keys = jax.random.split(key, 3)
    row_scale = jnp.exp(jax.random.uniform(keys[0], (SEQS, L, 1), jnp.float32, math.log(0.3), math.log(3.0)))
    col_scale = jnp.exp(jax.random.uniform(keys[1], (1, 1, C), jnp.float32, math.log(0.3), math.log(3.0)))
    base = jnp.clip(jax.random.normal(keys[2], (SEQS, L, C), jnp.float32), -4.0, 4.0)
    return (base * row_scale * col_scale).astype(jnp.bfloat16)


def levels(rng, shape, cuts, smallest, largest):
    loudness, own = 1.0, jax.random.fold_in(rng, 6)
    for dim, blocks in cuts:
        heights = jnp.exp(jax.random.uniform(jax.random.fold_in(own, dim), (blocks,), jnp.float32, smallest / len(cuts), largest / len(cuts)))
        loudness = loudness * jnp.repeat(heights, shape[dim] // blocks).reshape([-1 if axis == dim else 1 for axis in range(len(shape))])
    return loudness


def gaussian(key, dims, deviation, reach, cuts=(), held_as=jnp.bfloat16):
    factor_of = levels(key, dims, cuts, -0.22, 0.18) if cuts else 1.0
    array = jax.random.normal(key, dims, jnp.float32) * deviation * factor_of
    return jnp.minimum(jnp.maximum(array, -reach), reach).astype(held_as)


def setup_inputs(seed: int = 0, part: int = 0) -> dict:
    streams_of = jax.random.split(jax.random.key(seed), 9)
    part_splits = jax.random.split(jax.random.fold_in(streams_of[8], part), 9)
    tokens = draw_tokens(jax.random.fold_in(jax.random.fold_in(streams_of[8], part), 71), part)
    right_factor = gaussian(streams_of[1], (NBLK, BLK, BLK), BLK ** -0.5, 0.25, ((0, 16),))
    left_factor = gaussian(streams_of[2], (BLK, NBLK, NBLK), NBLK ** -0.5, 0.375, ((0, 16),))
    twiddle = jnp.clip(jnp.exp(math.log(2.0) - 1.3862944 * jax.random.uniform(streams_of[3], (NBLK, BLK), jnp.float32) ** levels(streams_of[3], (NBLK, BLK), ((0, 16),), -0.2, 0.2)), 0.5, 2.0)
    norm_gain = jnp.clip(1.0 + 0.18 * jax.random.normal(streams_of[4], (C,), jnp.float32), 0.1, 1.9)
    mix_gain = jnp.clip(1.0 + 0.18 * jax.random.normal(streams_of[5], (C,), jnp.float32), 0.1, 1.9)
    value_weight = gaussian(streams_of[6], (C, C), C ** -0.5, 0.21875)
    gate_weight = gaussian(streams_of[7], (C, C), C ** -0.5, 0.21875)
    return dict(tokens=tokens, right_factor=right_factor, left_factor=left_factor, twiddle=twiddle, norm_gain=norm_gain, mix_gain=mix_gain, value_weight=value_weight, gate_weight=gate_weight)


def rms_scale(values, gain):
    mean_square = lax.optimization_barrier(jnp.mean(values * values, axis=-1, keepdims=True))
    return values * jax.lax.rsqrt(mean_square + 1e-05) * gain

def reference(tokens, right_factor, left_factor, twiddle, norm_gain, mix_gain, value_weight, gate_weight):
    widened = tokens.astype(jnp.float32)
    normed = rms_scale(widened, norm_gain).astype(jnp.bfloat16)
    blocked = normed.reshape(SEQS, NBLK, BLK, C).astype(jnp.float32)
    section_one = jnp.einsum('ajb,sabc->sajc', right_factor.astype(jnp.float32), blocked)
    section_one = (section_one * twiddle[None, :, :, None]).astype(jnp.bfloat16)
    mixed = jnp.einsum('jia,sajc->sijc', left_factor.astype(jnp.float32), section_one.astype(jnp.float32))
    mixed = mixed.astype(jnp.bfloat16).reshape(SEQS, L, C)
    residual_sum = widened + mixed.astype(jnp.float32)
    mix_normed = rms_scale(residual_sum, mix_gain).astype(jnp.bfloat16).reshape(SEQS * L, C)
    values_out = jnp.dot(mix_normed, value_weight, preferred_element_type=jnp.float32)
    gates = jnp.dot(mix_normed, gate_weight, preferred_element_type=jnp.float32)
    gated = (values_out * jax.nn.sigmoid(gates)).reshape(SEQS, L, C)
    return (residual_sum + gated).astype(jnp.bfloat16)
```

```python
import functools

import jax
import jax.numpy as jnp
from jax import lax
from jax.experimental import pallas as pl
from jax.experimental.pallas import tpu as pltpu
from jax.sharding import PartitionSpec as P

MESH = pl.DeviceIdType.MESH
T = 16
GROUP = 2
HALVES = 2


def layer_kernel(
    n,
    tok_hbm, right_hbm, left_hbm, tw_ref, ngain_ref, mgain_ref, wv_hbm, wg_hbm,
    out_hbm,
    sbuf, r1, r2, tbuf, rbuf, nbuf, twt, lbuf, wv, wg, perm, kbuf, obuf,
    send1, recv1, send2, recv2, tsem, rsem, wsem, ksem, osem,
):
    me = lax.axis_index("seq")
    grp = lax.axis_index("grp")
    block_len = tbuf.shape[1]
    width = tbuf.shape[2]

    def load_block(a, slot):
        return (
            pltpu.make_async_copy(tok_hbm.at[a], tbuf.at[slot], tsem.at[slot]),
            pltpu.make_async_copy(right_hbm.at[a], rbuf.at[slot], rsem.at[slot]),
        )

    for copy in load_block(0, 0):
        copy.start()
    weights = [
        pltpu.make_async_copy(left_hbm, lbuf, wsem.at[0]),
        pltpu.make_async_copy(wv_hbm, wv, wsem.at[1]),
        pltpu.make_async_copy(wg_hbm, wg, wsem.at[2]),
    ]

    barrier = pltpu.get_barrier_semaphore()

    @pl.loop(1, n)
    def _(k):
        pl.semaphore_signal(
            barrier, inc=1, device_id=(grp, lax.rem(me + k, n)), device_id_type=MESH
        )

    row = lax.broadcasted_iota(jnp.int32, (T * T, T * T), 0)
    col = lax.broadcasted_iota(jnp.int32, (T * T, T * T), 1)
    swapped = (row % T) * T + row // T
    perm[...] = jnp.where(col == swapped, 1.0, 0.0).astype(jnp.bfloat16)
    twt[...] = tw_ref[...].T
    pl.semaphore_wait(barrier, n - 1)

    def first(a):
        slot = lax.rem(a, 2)
        for copy in load_block(a, slot):
            copy.wait()

        @pl.when(a + 1 < T)
        def _():
            for copy in load_block(a + 1, 1 - slot):
                copy.start()

        chunk = 64

        @pl.loop(0, block_len // chunk)
        def _(q):
            rows = pl.ds(pl.multiple_of(q * chunk, chunk), chunk)
            x = tbuf[slot, rows, :].astype(jnp.float32)
            scale = lax.rsqrt(jnp.mean(x * x, axis=-1, keepdims=True) + 1e-05)
            nbuf[rows, :] = (x * scale * ngain_ref[...]).astype(jnp.bfloat16)

        part = 256
        for q in range(block_len // part):
            rows = pl.ds(q * part, part)
            tw = twt[rows, :]
            lane = lax.broadcasted_iota(jnp.int32, tw.shape, 1)
            tw = jnp.sum(jnp.where(lane == a, tw, 0.0), axis=1, keepdims=True)
            s1 = jnp.dot(rbuf[slot, rows, :], nbuf[...], preferred_element_type=jnp.float32)
            s1 = (s1 * tw).astype(jnp.bfloat16).reshape(part // (T * HALVES), HALVES, T, width)
            for d in range(s1.shape[0]):
                for h in range(HALVES):
                    sbuf[h, q * s1.shape[0] + d, a] = s1[d, h]

    def send_first(h, k, a0, count):
        d = lax.rem(me + k, n)
        blocks = pl.ds(a0, count)
        pltpu.make_async_remote_copy(
            src_ref=sbuf.at[h, d, blocks],
            dst_ref=r1.at[h, me, blocks],
            send_sem=send1.at[h, k],
            recv_sem=recv1.at[h, me],
            device_id=(grp, d),
            device_id_type=MESH,
        ).start()

    @pl.loop(0, T // GROUP)
    def _(g):
        @pl.loop(0, GROUP)
        def _(u):
            first(g * GROUP + u)

        @pl.loop(1, n)
        def _(k):
            send_first(0, k, g * GROUP, GROUP)

        @pl.when(g == 0)
        def _():
            for copy in weights:
                copy.start()

    @pl.loop(1, HALVES)
    def _(h):
        @pl.loop(1, n)
        def _(k):
            send_first(h, k, 0, T)

    @pl.loop(0, HALVES)
    def _(h):
        pltpu.make_async_copy(sbuf.at[h, me], r1.at[h, me], recv1.at[h, me]).start()

    for copy in weights:
        copy.wait()

    @pl.loop(0, HALVES)
    def _(h):
        @pl.loop(0, n)
        def _(k):
            s = lax.rem(me + n - k, n)
            tile = r1.at[h, s]
            pltpu.make_async_copy(tile, tile, recv1.at[h, s]).wait()
            x = jnp.dot(
                perm[...], r1[h, s].reshape(T * T, width), preferred_element_type=jnp.float32
            )
            r1[h, s] = x.astype(jnp.bfloat16).reshape(T, T, width)

        @pl.loop(1, n)
        def _(k):
            tile = sbuf.at[h, 0]
            pltpu.make_async_copy(tile, tile, send1.at[h, k]).wait()

        @pl.loop(0, T)
        def _(j):
            x = r1[h, :, j].reshape(n * T, width)
            mixed = jnp.dot(lbuf[h * T + j], x, preferred_element_type=jnp.float32)
            sbuf[h, :, j] = mixed.astype(jnp.bfloat16).reshape(n, T, width)

        @pl.loop(1, n)
        def _(k):
            d = lax.rem(me + k, n)
            pltpu.make_async_remote_copy(
                src_ref=sbuf.at[h, d],
                dst_ref=r2.at[h, me],
                send_sem=send2.at[h, k],
                recv_sem=recv2.at[h, me],
                device_id=(grp, d),
                device_id_type=MESH,
            ).start()

        pltpu.make_async_copy(sbuf.at[h, me], r2.at[h, me], recv2.at[h, me]).start()

    def columns(t):
        h = t // n
        s = lax.rem(me + n - lax.rem(t, n), n)
        return h, s, pl.ds(pl.multiple_of((s * HALVES + h) * T, T), T)

    def load_tokens(t, slot):
        _, _, cols = columns(t)
        return pltpu.make_async_copy(tok_hbm.at[:, cols], kbuf.at[slot], ksem.at[slot])

    def store_out(t, slot):
        _, _, cols = columns(t)
        return pltpu.make_async_copy(obuf.at[slot], out_hbm.at[:, cols], osem.at[slot])

    load_tokens(0, 0).start()
    tiles = HALVES * n

    @pl.loop(0, tiles)
    def _(t):
        slot = lax.rem(t, 2)
        h, s, _ = columns(t)
        load_tokens(t, slot).wait()

        @pl.when(t + 1 < tiles)
        def _():
            load_tokens(t + 1, 1 - slot).start()

        tile = r2.at[h, s]
        pltpu.make_async_copy(tile, tile, recv2.at[h, s]).wait()
        mixed = jnp.dot(
            perm[...], r2[h, s].reshape(T * T, width), preferred_element_type=jnp.float32
        )
        res = kbuf[slot].reshape(T * T, width).astype(jnp.float32) + mixed
        scale = lax.rsqrt(jnp.mean(res * res, axis=-1, keepdims=True) + 1e-05)
        normed = (res * scale * mgain_ref[...]).astype(jnp.bfloat16)

        @pl.when(t >= 2)
        def _():
            store_out(t - 2, slot).wait()

        step = 256
        for c in range(0, width, step):
            cols = slice(c, c + step)
            v = jnp.dot(normed, wv[:, cols], preferred_element_type=jnp.float32)
            g = jnp.dot(normed, wg[:, cols], preferred_element_type=jnp.float32)
            out = res[:, cols] + v * jax.nn.sigmoid(g)
            obuf[slot, :, :, cols] = out.astype(jnp.bfloat16).reshape(T, T, step)
        store_out(t, slot).start()

    for t in (tiles - 2, tiles - 1):
        store_out(t, t % 2).wait()

    @pl.loop(0, HALVES)
    def _(h):
        @pl.loop(1, n)
        def _(k):
            tile = sbuf.at[h, 0]
            pltpu.make_async_copy(tile, tile, send2.at[h, k]).wait()


def fused_body(
    n, tokens, right_factor, left_factor, twiddle, norm_gain, mix_gain, value_weight, gate_weight
):
    _, rows_here, width = tokens.shape
    block_len = right_factor.shape[1]
    order = left_factor.shape[1]
    bf16, f32 = jnp.bfloat16, jnp.float32
    hbm = pl.BlockSpec(memory_space=pl.ANY)
    vmem = pl.BlockSpec(memory_space=pltpu.VMEM)
    dma = pltpu.SemaphoreType.DMA
    exchange = pltpu.VMEM((HALVES, n, T, T, width), bf16)
    out = pl.pallas_call(
        functools.partial(layer_kernel, n),
        out_shape=jax.ShapeDtypeStruct((T, block_len, width), bf16),
        in_specs=[hbm, hbm, hbm, vmem, vmem, vmem, hbm, hbm],
        out_specs=hbm,
        scratch_shapes=[
            exchange,
            exchange,
            exchange,
            pltpu.VMEM((2, block_len, width), bf16),
            pltpu.VMEM((2, block_len, block_len), bf16),
            pltpu.VMEM((block_len, width), bf16),
            pltpu.VMEM((block_len, T), f32),
            pltpu.VMEM((HALVES * T, order, order), bf16),
            pltpu.VMEM((width, width), bf16),
            pltpu.VMEM((width, width), bf16),
            pltpu.VMEM((T * T, T * T), bf16),
            pltpu.VMEM((2, T, T, width), bf16),
            pltpu.VMEM((2, T, T, width), bf16),
            dma((HALVES, n)),
            dma((HALVES, n)),
            dma((HALVES, n)),
            dma((HALVES, n)),
            dma((2,)),
            dma((2,)),
            dma((3,)),
            dma((2,)),
            dma((2,)),
        ],
        compiler_params=pltpu.CompilerParams(
            collective_id=0, has_side_effects=True, vmem_limit_bytes=58 * 2**20
        ),
    )(
        tokens.reshape(T, block_len, width),
        right_factor,
        left_factor,
        twiddle,
        norm_gain.reshape(1, width),
        mix_gain.reshape(1, width),
        value_weight,
        gate_weight,
    )
    return out.reshape(tokens.shape)


def rms_scale(values, gain):
    mean_square = jnp.mean(values * values, axis=-1, keepdims=True)
    return values * lax.rsqrt(mean_square + 1e-05) * gain


def second_section(columns, left_factor):
    mixed = jnp.einsum("jia,sajc->sijc", left_factor, columns, preferred_element_type=jnp.float32)
    return mixed.astype(jnp.bfloat16)


def body(
    tokens, right_factor, left_factor, twiddle, norm_gain, mix_gain, value_weight, gate_weight
):
    seqs_here, rows_here, width = tokens.shape
    blocks_here = right_factor.shape[0]
    block_len = right_factor.shape[1]
    n = lax.axis_size("seq")
    if seqs_here == 1 and blocks_here == T and n * T == left_factor.shape[1] and n * T * HALVES == block_len:
        return fused_body(
            n, tokens, right_factor, left_factor, twiddle, norm_gain, mix_gain, value_weight, gate_weight
        )
    widened = tokens.astype(jnp.float32)
    normed = rms_scale(widened, norm_gain).astype(jnp.bfloat16)
    blocked = normed.reshape(seqs_here, blocks_here, block_len, width)
    section_one = jnp.einsum(
        "ajb,sabc->sajc", right_factor, blocked, preferred_element_type=jnp.float32
    )
    section_one = (section_one * twiddle[None, :, :, None]).astype(jnp.bfloat16)
    columns = lax.all_to_all(section_one, "seq", split_axis=2, concat_axis=1, tiled=True)
    mixed_cols = second_section(columns, left_factor)
    mixed_back = lax.all_to_all(mixed_cols, "seq", split_axis=1, concat_axis=2, tiled=True)
    residual_sum = widened + mixed_back.reshape(seqs_here, rows_here, width).astype(jnp.float32)
    mix_normed = (
        rms_scale(residual_sum, mix_gain).astype(jnp.bfloat16).reshape(seqs_here * rows_here, width)
    )
    values_out = jnp.dot(mix_normed, value_weight, preferred_element_type=jnp.float32)
    gates = jnp.dot(mix_normed, gate_weight, preferred_element_type=jnp.float32)
    gated = (values_out * jax.nn.sigmoid(gates)).reshape(seqs_here, rows_here, width)
    return (residual_sum + gated).astype(jnp.bfloat16)


def solution(mesh):
    return jax.shard_map(
        body,
        mesh=mesh,
        in_specs=(
            P("grp", "seq", None),
            P("seq", None, None),
            P("seq", None, None),
            P("seq", None),
            P(),
            P(),
            P(),
            P(),
        ),
        out_specs=P("grp", "seq", None),
        check_vma=False,
    )
```

```python
import functools

import jax
import jax.numpy as jnp
from jax import lax
from jax.experimental import pallas as pl
from jax.experimental.pallas import tpu as pltpu
from jax.sharding import PartitionSpec as P

MESH = pl.DeviceIdType.MESH
T = 16
GROUP = 2
HALVES = 2


def layer_kernel(
    n,
    tok_hbm, right_hbm, left_hbm, tw_ref, ngain_ref, mgain_ref, wv_hbm, wg_hbm,
    out_hbm,
    sbuf, r1, r2, tbuf, rbuf, nbuf, twt, lbuf, wv, wg, perm, kbuf, obuf,
    send1, recv1, send2, recv2, tsem, rsem, wsem, ksem, osem,
):
    me = lax.axis_index("seq")
    grp = lax.axis_index("grp")
    block_len = tbuf.shape[1]
    width = tbuf.shape[2]

    def load_block(a, slot):
        return (
            pltpu.make_async_copy(tok_hbm.at[a], tbuf.at[slot], tsem.at[slot]),
            pltpu.make_async_copy(right_hbm.at[a], rbuf.at[slot], rsem.at[slot]),
        )

    for copy in load_block(0, 0):
        copy.start()
    weights = [
        pltpu.make_async_copy(left_hbm, lbuf, wsem.at[0]),
        pltpu.make_async_copy(wv_hbm, wv, wsem.at[1]),
        pltpu.make_async_copy(wg_hbm, wg, wsem.at[2]),
    ]

    barrier = pltpu.get_barrier_semaphore()

    @pl.loop(1, n)
    def _(k):
        pl.semaphore_signal(
            barrier, inc=1, device_id=(grp, lax.rem(me + k, n)), device_id_type=MESH
        )

    row = lax.broadcasted_iota(jnp.int32, (T * T, T * T), 0)
    col = lax.broadcasted_iota(jnp.int32, (T * T, T * T), 1)
    swapped = (row % T) * T + row // T
    perm[...] = jnp.where(col == swapped, 1.0, 0.0).astype(jnp.bfloat16)
    twt[...] = tw_ref[...].T
    pl.semaphore_wait(barrier, n - 1)

    def first(a):
        slot = lax.rem(a, 2)
        for copy in load_block(a, slot):
            copy.wait()

        @pl.when(a + 1 < T)
        def _():
            for copy in load_block(a + 1, 1 - slot):
                copy.start()

        chunk = 64

        @pl.loop(0, block_len // chunk)
        def _(q):
            rows = pl.ds(pl.multiple_of(q * chunk, chunk), chunk)
            x = tbuf[slot, rows, :].astype(jnp.float32)
            scale = lax.rsqrt(jnp.mean(x * x, axis=-1, keepdims=True) + 1e-05)
            nbuf[rows, :] = (x * scale * ngain_ref[...].reshape(1, width)).astype(jnp.bfloat16)

        part = 256
        for q in range(block_len // part):
            rows = pl.ds(q * part, part)
            tw = twt[rows, :]
            lane = lax.broadcasted_iota(jnp.int32, tw.shape, 1)
            tw = jnp.sum(jnp.where(lane == a, tw, 0.0), axis=1, keepdims=True)
            s1 = jnp.dot(rbuf[slot, rows, :], nbuf[...], preferred_element_type=jnp.float32)
            s1 = (s1 * tw).astype(jnp.bfloat16).reshape(part // (T * HALVES), HALVES, T, width)
            for d in range(s1.shape[0]):
                for h in range(HALVES):
                    sbuf[h, q * s1.shape[0] + d, a] = s1[d, h]

    def send_first(h, k, a0, count):
        d = lax.rem(me + k, n)
        blocks = pl.ds(a0, count)
        pltpu.make_async_remote_copy(
            src_ref=sbuf.at[h, d, blocks],
            dst_ref=r1.at[h, me, blocks],
            send_sem=send1.at[h, k],
            recv_sem=recv1.at[h, me],
            device_id=(grp, d),
            device_id_type=MESH,
        ).start()

    @pl.loop(0, T // GROUP)
    def _(g):
        @pl.loop(0, GROUP)
        def _(u):
            first(g * GROUP + u)

        @pl.loop(1, n)
        def _(k):
            send_first(0, k, g * GROUP, GROUP)

        @pl.when(g == 0)
        def _():
            for copy in weights:
                copy.start()

    @pl.loop(1, HALVES)
    def _(h):
        @pl.loop(1, n)
        def _(k):
            send_first(h, k, 0, T)

    @pl.loop(0, HALVES)
    def _(h):
        pltpu.make_async_copy(sbuf.at[h, me], r1.at[h, me], recv1.at[h, me]).start()

    for copy in weights:
        copy.wait()

    @pl.loop(0, HALVES)
    def _(h):
        @pl.loop(0, n)
        def _(k):
            s = lax.rem(me + n - k, n)
            tile = r1.at[h, s]
            pltpu.make_async_copy(tile, tile, recv1.at[h, s]).wait()
            x = jnp.dot(
                perm[...], r1[h, s].reshape(T * T, width), preferred_element_type=jnp.float32
            )
            r1[h, s] = x.astype(jnp.bfloat16).reshape(T, T, width)

        @pl.loop(1, n)
        def _(k):
            tile = sbuf.at[h, 0]
            pltpu.make_async_copy(tile, tile, send1.at[h, k]).wait()

        @pl.loop(0, T)
        def _(j):
            x = r1[h, :, j].reshape(n * T, width)
            mixed = jnp.dot(lbuf[h * T + j], x, preferred_element_type=jnp.float32)
            sbuf[h, :, j] = mixed.astype(jnp.bfloat16).reshape(n, T, width)

        @pl.loop(1, n)
        def _(k):
            d = lax.rem(me + k, n)
            pltpu.make_async_remote_copy(
                src_ref=sbuf.at[h, d],
                dst_ref=r2.at[h, me],
                send_sem=send2.at[h, k],
                recv_sem=recv2.at[h, me],
                device_id=(grp, d),
                device_id_type=MESH,
            ).start()

        pltpu.make_async_copy(sbuf.at[h, me], r2.at[h, me], recv2.at[h, me]).start()

    def columns(t):
        h = t // n
        s = lax.rem(me + n - lax.rem(t, n), n)
        return h, s, pl.ds(pl.multiple_of((s * HALVES + h) * T, T), T)

    def load_tokens(t, slot):
        _, _, cols = columns(t)
        return pltpu.make_async_copy(tok_hbm.at[:, cols], kbuf.at[slot], ksem.at[slot])

    def store_out(t, slot):
        _, _, cols = columns(t)
        return pltpu.make_async_copy(obuf.at[slot], out_hbm.at[:, cols], osem.at[slot])

    load_tokens(0, 0).start()
    tiles = HALVES * n

    @pl.loop(0, tiles)
    def _(t):
        slot = lax.rem(t, 2)
        h, s, _ = columns(t)
        load_tokens(t, slot).wait()

        @pl.when(t + 1 < tiles)
        def _():
            load_tokens(t + 1, 1 - slot).start()

        tile = r2.at[h, s]
        pltpu.make_async_copy(tile, tile, recv2.at[h, s]).wait()
        mixed = jnp.dot(
            perm[...], r2[h, s].reshape(T * T, width), preferred_element_type=jnp.float32
        )
        res = kbuf[slot].reshape(T * T, width).astype(jnp.float32) + mixed
        scale = lax.rsqrt(jnp.mean(res * res, axis=-1, keepdims=True) + 1e-05)
        normed = (res * scale * mgain_ref[...].reshape(1, width)).astype(jnp.bfloat16)

        @pl.when(t >= 2)
        def _():
            store_out(t - 2, slot).wait()

        step = 256
        for c in range(0, width, step):
            cols = slice(c, c + step)
            v = jnp.dot(normed, wv[:, cols], preferred_element_type=jnp.float32)
            g = jnp.dot(normed, wg[:, cols], preferred_element_type=jnp.float32)
            out = res[:, cols] + v * jax.nn.sigmoid(g)
            obuf[slot, :, :, cols] = out.astype(jnp.bfloat16).reshape(T, T, step)
        store_out(t, slot).start()

    for t in (tiles - 2, tiles - 1):
        store_out(t, t % 2).wait()

    @pl.loop(0, HALVES)
    def _(h):
        @pl.loop(1, n)
        def _(k):
            tile = sbuf.at[h, 0]
            pltpu.make_async_copy(tile, tile, send2.at[h, k]).wait()


def fused_body(
    n, tokens, right_factor, left_factor, twiddle, norm_gain, mix_gain, value_weight, gate_weight
):
    _, rows_here, width = tokens.shape
    block_len = right_factor.shape[1]
    order = left_factor.shape[1]
    bf16, f32 = jnp.bfloat16, jnp.float32
    hbm = pl.BlockSpec(memory_space=pl.ANY)
    vmem = pl.BlockSpec(memory_space=pltpu.VMEM)
    dma = pltpu.SemaphoreType.DMA
    exchange = pltpu.VMEM((HALVES, n, T, T, width), bf16)
    out = pl.pallas_call(
        functools.partial(layer_kernel, n),
        out_shape=jax.ShapeDtypeStruct((T, block_len, width), bf16),
        in_specs=[hbm, hbm, hbm, vmem, vmem, vmem, hbm, hbm],
        out_specs=hbm,
        scratch_shapes=[
            exchange,
            exchange,
            exchange,
            pltpu.VMEM((2, block_len, width), bf16),
            pltpu.VMEM((2, block_len, block_len), bf16),
            pltpu.VMEM((block_len, width), bf16),
            pltpu.VMEM((block_len, T), f32),
            pltpu.VMEM((HALVES * T, order, order), bf16),
            pltpu.VMEM((width, width), bf16),
            pltpu.VMEM((width, width), bf16),
            pltpu.VMEM((T * T, T * T), bf16),
            pltpu.VMEM((2, T, T, width), bf16),
            pltpu.VMEM((2, T, T, width), bf16),
            dma((HALVES, n)),
            dma((HALVES, n)),
            dma((HALVES, n)),
            dma((HALVES, n)),
            dma((2,)),
            dma((2,)),
            dma((3,)),
            dma((2,)),
            dma((2,)),
        ],
        compiler_params=pltpu.CompilerParams(
            collective_id=0, has_side_effects=True, vmem_limit_bytes=58 * 2**20
        ),
    )(
        tokens.reshape(T, block_len, width),
        right_factor,
        left_factor,
        twiddle,
        norm_gain,
        mix_gain,
        value_weight,
        gate_weight,
    )
    return out.reshape(tokens.shape)


def rms_scale(values, gain):
    mean_square = jnp.mean(values * values, axis=-1, keepdims=True)
    return values * lax.rsqrt(mean_square + 1e-05) * gain


def second_section(columns, left_factor):
    mixed = jnp.einsum("jia,sajc->sijc", left_factor, columns, preferred_element_type=jnp.float32)
    return mixed.astype(jnp.bfloat16)


def body(
    tokens, right_factor, left_factor, twiddle, norm_gain, mix_gain, value_weight, gate_weight
):
    seqs_here, rows_here, width = tokens.shape
    blocks_here = right_factor.shape[0]
    block_len = right_factor.shape[1]
    n = lax.axis_size("seq")
    if seqs_here == 1 and blocks_here == T and n * T == left_factor.shape[1] and n * T * HALVES == block_len:
        return fused_body(
            n, tokens, right_factor, left_factor, twiddle, norm_gain, mix_gain, value_weight, gate_weight
        )
    widened = tokens.astype(jnp.float32)
    normed = rms_scale(widened, norm_gain).astype(jnp.bfloat16)
    blocked = normed.reshape(seqs_here, blocks_here, block_len, width)
    section_one = jnp.einsum(
        "ajb,sabc->sajc", right_factor, blocked, preferred_element_type=jnp.float32
    )
    section_one = (section_one * twiddle[None, :, :, None]).astype(jnp.bfloat16)
    columns = lax.all_to_all(section_one, "seq", split_axis=2, concat_axis=1, tiled=True)
    mixed_cols = second_section(columns, left_factor)
    mixed_back = lax.all_to_all(mixed_cols, "seq", split_axis=1, concat_axis=2, tiled=True)
    residual_sum = widened + mixed_back.reshape(seqs_here, rows_here, width).astype(jnp.float32)
    mix_normed = (
        rms_scale(residual_sum, mix_gain).astype(jnp.bfloat16).reshape(seqs_here * rows_here, width)
    )
    values_out = jnp.dot(mix_normed, value_weight, preferred_element_type=jnp.float32)
    gates = jnp.dot(mix_normed, gate_weight, preferred_element_type=jnp.float32)
    gated = (values_out * jax.nn.sigmoid(gates)).reshape(seqs_here, rows_here, width)
    return (residual_sum + gated).astype(jnp.bfloat16)


def solution(mesh):
    return jax.shard_map(
        body,
        mesh=mesh,
        in_specs=(
            P("grp", "seq", None),
            P("seq", None, None),
            P("seq", None, None),
            P("seq", None),
            P(),
            P(),
            P(),
            P(),
        ),
        out_specs=P("grp", "seq", None),
        check_vma=False,
    )
```
